256 devices in a mesh: rows: 32 (over x_hi, z, core), cols: 8 (over y, x_lo).
Axes of the slice: x: 4 (x_hi: 2, x_lo: 2; x = x_hi * 2 + x_lo), y: 4, z: 8, core: 2. Of those that a mesh axis runs over, the one named last changes fastest.
Arguments:
- image_tokens: bfloat16 [32, 32, 32, 1024], P('rows', None, 'cols'), may hold values from -1.1953125 to 1.1953125
- cotangent: bfloat16 [32, 32, 32, 1024], P('rows', None, 'cols'), may hold values from -6 to 6
- noise_level: int32 [32], P('rows'), may hold values from 0 to 255
- cond_table: float32 [256, 1024], replicated, may hold values from 0.1 to 1.9
- head_scale: float32 [16], replicated, may hold values from 2 to 12
- w_qkv: bfloat16 [3, 1024, 1024], P(None, 'rows', 'cols'), may hold values from -0.1875 to 0.1875
- w_out: bfloat16 [1024, 1024], P('cols', 'rows'), may hold values from -0.1875 to 0.1875
Outputs:
- output_tokens: bfloat16 [32, 32, 32, 1024], P('rows', None, 'cols')
- grad_tokens: bfloat16 [32, 32, 32, 1024], P('rows', None, 'cols')
- grad_w_qkv: float32 [3, 1024, 1024], P(None, 'rows', 'cols')
- grad_w_out: float32 [1024, 1024], P('cols', 'rows')
The draws below stay inside these ranges and needn't reach their ends.
All inputs are finite; a program needn't handle non-finite values.
Results may differ from the reference program's by a relative error of at most 0.024.
Values may be sent and summed in bfloat16 or wider, within the bound.
A program may use at most 64 MiB of HBM per device.

```python
import math
import jax
import jax.numpy as jnp
from jax import lax

D = 1024
HEADS = 16
HDIM = 64
LEVELS = 256
NH = 32
NW = 32
BATCH = 32


def plant(drawn, own_key, least, largest):
    place = [jax.random.randint(jax.random.fold_in(own_key, axis), (), 0, length) for axis, length in enumerate(drawn.shape)]
    longest = drawn.shape.index(max(drawn.shape))
    next_to = place[:longest] + [(place[longest] + 1) % drawn.shape[longest]] + place[longest + 1:]
    return drawn.at[tuple(place)].set(least).at[tuple(next_to)].set(largest)


def block_scale(own_key, shape, cuts, low, largest):
    def one(position, parts):
        draws = jax.random.uniform(jax.random.fold_in(jax.random.fold_in(own_key, 6), position), (parts,), jnp.float32, low / len(cuts), largest / len(cuts))
        return jnp.repeat(jnp.exp(draws), shape[position] // parts).reshape((-1,) + (1,) * (len(shape) - position - 1))

    factor_of = one(*cuts[0])
    for cut in cuts[1:]:
        factor_of = factor_of * one(*cut)
    return factor_of


def centred(rng, extent, spread, bound, shards=(), held_as=jnp.bfloat16):
    factor_of = block_scale(rng, extent, shards, -0.22, 0.18) if shards else 1.0
    entries = jax.random.normal(rng, extent, jnp.float32) * spread * factor_of
    return jnp.minimum(jnp.maximum(entries, -bound), bound).astype(held_as)


def setup_inputs(seed: int = 0) -> dict:
    key_list = jax.random.split(jax.random.key(seed), 8)
    image_tokens = centred(key_list[0], (BATCH, NH, NW, D), 0.2, 1.1953125, ((0, 32), (2, 8)))
    cotangent = centred(key_list[1], (BATCH, NH, NW, D), 1.0, 6.0, ((0, 32), (2, 8)))
    noise_level = plant(jax.random.randint(key_list[2], (BATCH,), 0, LEVELS), jax.random.fold_in(key_list[2], 1), 0, LEVELS - 1).astype(jnp.int32)
    cond_table = jnp.clip(1.0 + 0.18 * jax.random.normal(key_list[3], (LEVELS, D), jnp.float32), 0.1, 1.9)
    head_scale = jnp.clip(jnp.exp(jax.random.uniform(key_list[4], (HEADS,), jnp.float32, math.log(2.0), math.log(12.0))), 2.0, 12.0)
    w_qkv = centred(key_list[5], (3, D, D), D ** -0.5, 0.1875, ((1, 32), (2, 8)))
    w_out = centred(key_list[6], (D, D), D ** -0.5, 0.1875, ((0, 8), (1, 32)))
    return {"image_tokens": image_tokens, "cotangent": cotangent, "noise_level": noise_level, "cond_table": cond_table, "head_scale": head_scale, "w_qkv": w_qkv, "w_out": w_out}


EPS = 1e-06

def rms_scale(values, gain):
    return values * lax.rsqrt(lax.optimization_barrier(jnp.mean(values * values, -1, keepdims=True)) + EPS) * gain

def unit_rows(query, keys, vals, scale, heads):
    count = query.shape[0]
    q_three = query.reshape(count, heads, -1)
    k_three = keys.reshape(count, heads, -1)
    q_unit = scale[None, :, None] * q_three / jnp.sqrt(lax.optimization_barrier(jnp.sum(q_three * q_three, -1, keepdims=True)) + EPS)
    k_unit = k_three / jnp.sqrt(lax.optimization_barrier(jnp.sum(k_three * k_three, -1, keepdims=True)) + EPS)
    return (q_unit.reshape(count, -1), k_unit.reshape(count, -1), vals)

def one_head(inputs):
    q_head, k_head, v_head, da_head = inputs
    scores = jnp.dot(q_head, k_head.T, preferred_element_type=jnp.float32)
    expo = jnp.exp(scores)
    den = lax.optimization_barrier(jnp.sum(expo, -1))
    inv_den = (1.0 / den).astype(jnp.bfloat16)
    inv_f = inv_den.astype(jnp.float32)[:, None]
    num = jnp.dot(expo.astype(jnp.bfloat16), v_head, preferred_element_type=jnp.float32)
    attn = (num * inv_f).astype(jnp.bfloat16)
    delta = lax.optimization_barrier(jnp.sum(da_head.astype(jnp.float32) * attn.astype(jnp.float32), -1))
    weights = expo * inv_f
    d_prob = jnp.dot(da_head, v_head.T, preferred_element_type=jnp.float32)
    d_score = (weights * (d_prob - delta[:, None])).astype(jnp.bfloat16)
    w_bf = weights.astype(jnp.bfloat16)
    d_q = jnp.dot(d_score, k_head, preferred_element_type=jnp.float32)
    d_k = jnp.dot(d_score.T, q_head, preferred_element_type=jnp.float32)
    d_v = jnp.dot(w_bf.T, da_head, preferred_element_type=jnp.float32)
    return (attn, d_q, d_k, d_v)

def image_pass(x_img, g_img, level, cond_table, head_scale, w_qkv, w_out):
    total = NH * NW
    x_flat = x_img.reshape(total, D).astype(jnp.float32)
    g_flat = g_img.reshape(total, D)
    pick = (jnp.arange(LEVELS, dtype=jnp.int32) == level)[:, None]
    gain = lax.optimization_barrier(jnp.sum(jnp.where(pick, cond_table, jnp.zeros_like(cond_table)), 0))
    normed = rms_scale(x_flat, gain).astype(jnp.bfloat16)
    query = jnp.dot(normed, w_qkv[0], preferred_element_type=jnp.float32)
    keys = jnp.dot(normed, w_qkv[1], preferred_element_type=jnp.float32)
    vals = jnp.dot(normed, w_qkv[2], preferred_element_type=jnp.float32)

    def unit_fn(a, b, c):
        return unit_rows(a, b, c, head_scale, HEADS)
    units, unit_back = jax.vjp(unit_fn, query, keys, vals)
    q_bf, k_bf, v_bf = [u.astype(jnp.bfloat16) for u in units]
    dattn = jnp.dot(g_flat, w_out.T, preferred_element_type=jnp.float32).astype(jnp.bfloat16)

    def by_head(arr):
        return arr.reshape(total, HEADS, HDIM).transpose(1, 0, 2)
    attn, d_q, d_k, d_v = lax.map(one_head, (by_head(q_bf), by_head(k_bf), by_head(v_bf), by_head(dattn)))

    def flat(arr):
        return arr.transpose(1, 0, 2).reshape(total, D)
    attn = flat(attn)
    out = jnp.dot(attn, w_out, preferred_element_type=jnp.float32)
    output_tokens = (x_flat + out).astype(jnp.bfloat16)
    grad_out_img = jnp.dot(attn.T, g_flat, preferred_element_type=jnp.float32)
    grads = unit_back((flat(d_q), flat(d_k), flat(d_v)))
    gproj = [gr.astype(jnp.bfloat16) for gr in grads]
    grad_qkv_img = jnp.stack([jnp.dot(normed.T, gp, preferred_element_type=jnp.float32) for gp in gproj])
    dnormed = jnp.dot(gproj[0], w_qkv[0].T, preferred_element_type=jnp.float32)
    dnormed = dnormed + jnp.dot(gproj[1], w_qkv[1].T, preferred_element_type=jnp.float32)
    dnormed = dnormed + jnp.dot(gproj[2], w_qkv[2].T, preferred_element_type=jnp.float32)
    _, norm_back = jax.vjp(lambda val: rms_scale(val, gain), x_flat)
    grad_tokens = (g_flat.astype(jnp.float32) + norm_back(dnormed)[0]).astype(jnp.bfloat16)
    return (output_tokens.reshape(NH, NW, D), grad_tokens.reshape(NH, NW, D), grad_qkv_img, grad_out_img)

def reference(image_tokens, cotangent, noise_level, cond_table, head_scale, w_qkv, w_out):

    def step(carry, item):
        x_img, g_img, level = item
        out, gtok, gq, go = image_pass(x_img, g_img, level, cond_table, head_scale, w_qkv, w_out)
        return ((carry[0] + gq, carry[1] + go), (out, gtok))
    init = (jnp.zeros((3, D, D), jnp.float32), jnp.zeros((D, D), jnp.float32))
    sums, stacked = lax.scan(step, init, (image_tokens, cotangent, noise_level))
    return (stacked[0], stacked[1], sums[0], sums[1])
```

```python
import jax
import jax.numpy as jnp
from jax import lax
from jax.experimental import pallas as pl
from jax.experimental.pallas import tpu as pltpu
from jax.sharding import PartitionSpec as P

EPS = 1e-06
LOG2E = 1.4426950408889634
MESH = pl.DeviceIdType.MESH
F32 = jnp.float32
BF16 = jnp.bfloat16
NSEM = 180
OWN = {(0, 128): (256, 384), (0, 256): (0, 256), (256, 384): (384, 512)}


def dot(a, b):
    return jnp.dot(a, b, preferred_element_type=F32)


def dot_nt(a, b):
    return lax.dot_general(a, b, (((1,), (1,)), ((), ())), preferred_element_type=F32)


def kernel(
    hs_ref, x_ref, g_ref, gain_ref, wqkv_ref, wout_ref,
    out_ref, gtok_ref, gqkv_ref, gout_ref,
    xs, n_all, g_two, n_t, wa, wb, wc,
    u_t, r_t, kq_t, kz, kq, v_x, v_t, p_all, attn, inv, ext, da_send, da_in,
    go_f, go_send, go_half, go_in,
    dk_t, dq_t, gp, a_in, g_in, part_own, part_send, part_in,
    gw_f, gw_b, gw_sib, gw_sum, gw_in, held,
    send_sem, recv_sem,
):
    r = lax.axis_index("rows")
    c = lax.axis_index("cols")
    y, xl = c // 2, c % 2
    xh, z, core = r // 16, (r // 2) % 8, r % 2
    m16 = r // 2

    def at_cols(yy, xx):
        return {"rows": r, "cols": yy * 2 + xx}

    def at_rows(xx, zz, cc):
        return {"rows": (xx * 8 + zz) * 2 + cc, "cols": c}

    yp, ym, yf = (y + 1) % 4, (y + 3) % 4, (y + 2) % 4
    up, down, side = at_cols(yp, xl), at_cols(ym, xl), at_cols(y, 1 - xl)
    zup, zdown = at_rows(xh, (z + 1) % 8, core), at_rows(xh, (z + 7) % 8, core)
    sib, over = at_rows(xh, z, 1 - core), at_rows(1 - xh, z, core)

    sends = []
    count = [0]

    def copy_of(k, src, dst, dev):
        return pltpu.make_async_remote_copy(
            src_ref=src, dst_ref=dst, send_sem=send_sem.at[k], recv_sem=recv_sem.at[k],
            device_id=dev, device_id_type=MESH,
        )

    def push(src, dst, dev):
        k = count[0]
        count[0] += 1
        d = copy_of(k, src, dst, dev)
        d.start()
        sends.append(d)
        return k

    def send(ref, dev):
        return push(ref, ref, dev)

    def arrive(k, ref):
        copy_of(k, ref, ref, side).wait_recv()

    barrier = pltpu.get_barrier_semaphore()
    peers = [at_cols((y + i) % 4, xl) for i in (1, 2, 3)]
    peers += [side, sib]
    peers += [{"rows": ((m16 + i) % 16) * 2 + core, "cols": c} for i in range(1, 16)]
    for dev in peers:
        pl.semaphore_signal(barrier, inc=1, device_id=dev, device_id_type=MESH)

    xf = x_ref[0].astype(F32).reshape(128, 1024)
    xs[...] = xf
    rs = lax.rsqrt(jnp.mean(xf * xf, -1, keepdims=True) + EPS)
    gain = gain_ref[...]
    n_all[c] = (xf * rs * gain).astype(BF16).reshape(2, 4, 16, 1024)
    g_two[xl] = g_ref[0].astype(F32).reshape(128, 1024).astype(BF16)
    wq, wk = wqkv_ref[0], wqkv_ref[1]
    wa[0, xh, z, core] = jnp.concatenate(
        [wqkv_ref[2], wk[:, :64], wq[:, :64], wout_ref[...], wk[:, 64:], wq[:, 64:]], -1
    )
    kz[...] = jnp.zeros_like(kz)
    pl.semaphore_wait(barrier, len(peers))

    k_over = send(wa.at[0, xh, z, core], over)

    def to_rows(buf, x_from, other, pieces):
        keys = []
        for i in (1, 2, 3):
            for src, dst in pieces:
                k = push(
                    wa.at[0, x_from, z, core, :, src[0]:src[1]],
                    buf.at[3 - i, x_from, z, core, :, dst[0]:dst[1]],
                    at_cols((y + i) % 4, xl),
                )
                keys.append((k, buf.at[3 - i, (xh + other) % 2, z, core, :, dst[0]:dst[1]]))
        return keys

    def come(keys):
        for k, ref in keys:
            arrive(k, ref)

    out_piece = [((256, 384), (0, 128))]
    qkv_pieces = [((0, 256), (0, 256)), ((384, 512), (256, 384))]
    b_keys = to_rows(wb, xh, 0, out_piece)

    def slot(yy, xx):
        return yy * 2 + xx

    def stage_two(buf, ks):
        k_side, k_up, k_down = ks
        below, above, next_to = slot(ym, xl), slot(yp, xl), slot(y, 1 - xl)
        arrive(k_up, buf.at[below])
        b0 = send(buf.at[below, 0], up)
        b1 = send(buf.at[below, :, 3], side)
        arrive(k_down, buf.at[above])
        a0 = send(buf.at[above, 1], down)
        a1 = send(buf.at[above, :, 3], side)
        arrive(k_side, buf.at[next_to])
        s0 = send(buf.at[next_to, :, 0:3], up)
        s1 = send(buf.at[next_to, :, 0:3], down)
        return b0, b1, a0, a1, s0, s1

    def stage_three(buf, ks):
        b0, b1, a0, a1, s0, s1 = ks
        far, below, above = slot(yf, xl), slot(ym, 1 - xl), slot(yp, 1 - xl)
        arrive(b0, buf.at[far, 0])
        f0 = send(buf.at[far, 0, 3], side)
        arrive(a0, buf.at[far, 1])
        f1 = send(buf.at[far, 1, 3], side)
        arrive(s0, buf.at[below, :, 0:3])
        e0 = send(buf.at[below, 0, 0:3], up)
        arrive(s1, buf.at[above, :, 0:3])
        e1 = send(buf.at[above, 1, 0:3], down)
        return b1, a1, f0, f1, e0, e1

    def stage_four(buf, ks):
        b1, a1, f0, f1, e0, e1 = ks
        far = slot(yf, 1 - xl)
        arrive(b1, buf.at[slot(ym, 1 - xl), :, 3])
        arrive(a1, buf.at[slot(yp, 1 - xl), :, 3])
        arrive(e0, buf.at[far, 0, 0:3])
        arrive(e1, buf.at[far, 1, 0:3])
        arrive(f0, buf.at[far, 0, 3])
        arrive(f1, buf.at[far, 1, 3])

    def turned(yy):
        def one(j, carry):
            s = 2 * yy + j
            n_t[:, pl.ds(pl.multiple_of(s * 128, 128), 128)] = n_all[s].reshape(128, 1024).T
            return carry
        lax.fori_loop(0, 2, one, 0)

    n_own = n_all.at[c]
    n_keys = send(n_own, side), send(n_own, up), send(n_own, down)

    class OverZ:
        def __init__(self, buf):
            self.buf = buf
            own = self.block(0)
            self.near = [send(own, self.to(d)) for d in (2, -2, 1, -1)]

        def to(self, d):
            return at_rows(xh, (z + 8 + d) % 8, core)

        def block(self, d):
            return self.buf.at[:, :, (z + 8 + d) % 8, core]

        def half(self, d, h):
            return self.buf.at[:, h, (z + 8 + d) % 8, core]

        def forward(self):
            self.far = []
            for k, d, h in ((self.near[0], -2, 0), (self.near[1], 2, 1)):
                arrive(k, self.block(d))
                one = 1 if d < 0 else -1
                self.far.append(send(self.block(d), self.to(one)))
                self.far.append(send(self.half(d, h), self.to(2 * one)))

        def to_sib(self):
            arrive(self.near[2], self.block(-1))
            arrive(self.near[3], self.block(1))
            arrive(self.far[0], self.block(-3))
            arrive(self.far[2], self.block(3))
            arrive(self.far[1], self.half(4, 0))
            arrive(self.far[3], self.half(4, 1))
            self.k_sib = send(self.buf.at[:, :, :, core], sib)

        def finish(self):
            arrive(self.k_sib, self.buf.at[:, :, :, 1 - core])

    class Ring:
        def __init__(self, buf):
            self.buf = buf
            self.sib_keys = []
            self.up, self.down = send(self.block(z), zup), send(self.block(z), zdown)
            self.to_sib(z)

        def block(self, zz):
            return self.buf.at[:, :, zz, core]

        def half(self, zz, h):
            return self.buf.at[:, h, zz, core]

        def to_sib(self, zz):
            self.sib_keys.append((send(self.block(zz), sib), zz))

        def step(self, d):
            lo, hi = (z + 8 - d) % 8, (z + d) % 8
            arrive(self.up, self.block(lo))
            self.up = send(self.block(lo) if d < 3 else self.half(lo, 0), zup)
            self.to_sib(lo)
            arrive(self.down, self.block(hi))
            self.down = send(self.block(hi) if d < 3 else self.half(hi, 1), zdown)
            self.to_sib(hi)

        def last(self):
            opp = (z + 4) % 8
            arrive(self.up, self.half(opp, 0))
            arrive(self.down, self.half(opp, 1))
            self.to_sib(opp)

        def finish(self):
            for k, zz in self.sib_keys:
                arrive(k, self.buf.at[:, :, zz, 1 - core])

    arrive(k_over, wa.at[0, 1 - xh, z, core])
    za = OverZ(wa)
    b_keys += to_rows(wb, 1 - xh, 1, out_piece)
    come(b_keys)
    zb = OverZ(wb)
    za.forward()
    n_keys = stage_two(n_all, n_keys)
    k_g = send(g_two.at[xl], side)
    zb.forward()
    za.to_sib()
    turned(y)
    n_keys = stage_three(n_all, n_keys)
    zb.to_sib()
    za.finish()

    sc = [hs_ref[c * 2], hs_ref[c * 2 + 1]]
    lane = lax.broadcasted_iota(jnp.int32, (256, 128), 1)
    first = lane < 64
    ones = [
        jnp.where((lane == 64) | (lane == 65), 1.0, 0.0),
        jnp.where(lane < 2, 1.0, 0.0),
    ]

    def rows_of(i):
        return pl.ds(pl.multiple_of(i * 256, 256), 256)

    def project(i):
        rows = rows_of(i)
        n = n_all[pl.ds(2 * i, 2)].reshape(256, 1024)
        w = wa[0].reshape(1024, 512)
        res = dot(n, jnp.concatenate([w[:, :256], w[:, 384:]], -1))
        vv = res[:, :128]
        for h in (0, 1):
            t = res[:, 128 + 128 * h:256 + 128 * h].T.reshape(2, 64, 256)
            rn = lax.rsqrt(jnp.sum(t * t, 1, keepdims=True) + EPS)
            t = t * rn
            u_t[h, :, :, rows] = t
            r_t[h, 0, :, rows] = rn[0]
            r_t[h, 1, :, rows] = rn[1] * sc[h]
            both = jnp.concatenate([t[0], t[1] * (sc[h] * LOG2E)], 0)
            kq_t[h, :, rows] = both.astype(BF16)
            kz[h, 64:128, rows] = t[0].astype(BF16)
            kq[h, rows] = both.T.astype(BF16)
            vx = jnp.where(first if h == 0 else ~first, vv, ones[h]).astype(BF16)
            v_x[h, rows] = vx
            v_t[h, :, rows] = vx.T

    def project_rest(j, carry):
        project((y + j) % 4)
        return carry

    project(y)
    stage_four(n_all, n_keys)
    c_keys = to_rows(wc, xh, 0, qkv_pieces) + to_rows(wc, 1 - xh, 1, qkv_pieces)
    lax.fori_loop(1, 4, project_rest, 0)

    zb.finish()
    arrive(k_g, g_two.at[1 - xl])
    gg = g_two[...].reshape(256, 1024)
    for a in (0, 2):
        w0 = wa[0, :, :, :, :, 256:384] if a == 0 else wb[a - 1]
        w = jnp.concatenate([w0.reshape(1024, 128), wb[a].reshape(1024, 128)], -1)
        t = dot(gg, w).astype(BF16)
        da_send[a] = t[:, :128].reshape(2, 128, 128)
        da_send[a + 1] = t[:, 128:].reshape(2, 128, 128)
    da_keys = []
    for i in (1, 2, 3):
        dst = da_in.at[pl.ds(2 * y, 2)]
        da_keys.append((push(da_send.at[i], dst, at_cols((y + i) % 4, xl)), (y + 4 - i) % 4))
    da_in[pl.ds(2 * y, 2)] = da_send[0]

    lane5 = lax.broadcasted_iota(jnp.int32, (512, 128), 1)

    def forward(i):
        rows = pl.ds(i * 512, 512)
        outs = []
        for h in (0, 1):
            s = dot(kq[h, rows], kz[h])
            p = jnp.exp2(s).astype(BF16)
            p_all[h, rows] = p
            num = dot(p, v_x[h])
            den = num[:, 64:65] if h == 0 else num[:, 0:1]
            iv = (1.0 / den).astype(BF16).astype(F32)
            inv[h, rows] = iv
            outs.append(num * iv)
        attn[pl.ds(4 * i, 4)] = jnp.where(lane5 < 64, outs[0], outs[1]).astype(BF16).reshape(
            4, 128, 128
        )

    forward(0)
    come(c_keys)
    forward(1)

    def spread(buf, into, lo):
        keys = []
        lanes = slice(lo, lo + 128)
        for i in (1, 2, 3):
            to = (y + i) % 4
            src = buf.at[pl.ds(2 * to, 2), :, lanes]
            keys.append((push(src, into.at[4 - i, :, :, lanes], at_cols(to, xl)), 4 - i))
        into[0, :, :, lanes] = buf[pl.ds(2 * y, 2), :, lanes]
        return keys

    def gathered(keys, into, lo):
        for k, rel in keys:
            arrive(k, into.at[rel, :, :, lo:lo + 128])

    a_keys = spread(attn, a_in, 0)
    zc = Ring(wc)
    for j in (1, 2, 3):
        turned((y + j) % 4)

    for k, frm in da_keys:
        arrive(k, da_in.at[pl.ds(2 * frm, 2)])

    def cot(i, carry):
        rows = rows_of(i)
        dd = da_in[pl.ds(2 * i, 2)].reshape(256, 128).astype(F32)
        prod = dd * attn[pl.ds(2 * i, 2)].reshape(256, 128).astype(F32)
        for h in (0, 1):
            iv = inv[h, rows]
            mine = first if h == 0 else ~first
            delta = jnp.sum(jnp.where(mine, prod, 0.0), -1, keepdims=True) * iv
            hi = delta.astype(BF16).astype(F32)
            lo = delta - hi
            at = 64 if h == 0 else 0
            e = jnp.where(mine, dd * iv, jnp.where(lane == at, -hi, jnp.where(lane == at + 1, -lo, 0.0)))
            ext[h, rows] = e.astype(BF16)
        return carry

    lax.fori_loop(0, 4, cot, 0)
    dvs = []
    for h in (0, 1):
        e_t = ext[h].T
        dvs.append(dot(e_t[64 * h:64 * h + 64], p_all[h]))
    gp[:, :, 0:128] = jnp.concatenate(dvs, 0).T.astype(BF16).reshape(8, 128, 128)
    v_keys = spread(gp, g_in, 0)

    def keep_grad(i, res, lo):
        gw_f[pl.ds(4 * i, 4), :, :, lo:lo + 128] = res.reshape(4, 2, 32, 128)
        gw_b[pl.ds(4 * i, 4), :, :, lo:lo + 128] = res.astype(BF16).reshape(4, 2, 32, 128)

    def weight_grad(lo, to):
        def one(i, carry):
            rhs = gp[:, :, lo:lo + 128].reshape(1024, 128)
            keep_grad(i, dot(n_t[rows_of(i), :], rhs), to)
            return carry
        lax.fori_loop(0, 4, one, 0)

    def out_grad_send():
        gg = g_two[...].reshape(256, 1024)
        for i in (2, 1, 3, 0):
            go = dot(a_in[i].reshape(256, 128).T, gg)
            go_f[i] = go
            if i == 2:
                go_send[2] = go.astype(BF16)
                keys = [
                    push(go_send.at[2, 0:64], go_half.at[0], up),
                    push(go_send.at[2, 64:128], go_half.at[1], down),
                ]
        return keys

    def out_grad_on(keys):
        arrive(keys[0], go_half.at[0])
        arrive(keys[1], go_half.at[1])
        go_send[0, 0:64] = (go_f[1, 0:64] + go_half[0].astype(F32)).astype(BF16)
        go_send[0, 64:128] = go_f[1, 64:128].astype(BF16)
        go_send[1, 0:64] = go_f[3, 0:64].astype(BF16)
        go_send[1, 64:128] = (go_f[3, 64:128] + go_half[1].astype(F32)).astype(BF16)
        return push(go_send.at[0], go_in.at[0], up), push(go_send.at[1], go_in.at[1], down)

    def out_grad(keys):
        arrive(keys[0], go_in.at[0])
        arrive(keys[1], go_in.at[1])
        for i in range(4):
            cols = slice(256 * i, 256 * i + 256)
            tot = go_f[0, :, cols] + go_in[0, :, cols].astype(F32) + go_in[1, :, cols].astype(F32)
            keep_grad(i, tot.T, 256)

    def pair_send(lo, hi):
        return push(gw_b.at[:, 1 - core, :, lo:hi], gw_sib.at[:, :, lo:hi], sib)

    def reduce_send(k, lo, hi):
        arrive(k, gw_sib.at[:, :, lo:hi])
        tot = gw_f[:, core, :, lo:hi] + gw_sib[:, :, lo:hi].astype(F32)
        gw_f[:, core, :, lo:hi] = tot
        gw_sum[:, :, lo:hi] = tot.astype(BF16)
        keys = []
        for i in range(1, 16):
            to = (m16 + i) % 16
            dev = {"rows": to * 2 + core, "cols": c}
            keys.append(
                (push(gw_sum.at[to, :, lo:hi], gw_in.at[m16, :, lo:hi], dev), (m16 + 16 - i) % 16)
            )
        return keys

    def reduce_done(keys, lo, hi):
        tot = gw_f[m16, core, :, lo:hi]
        for k, frm in keys:
            arrive(k, gw_in.at[frm, :, lo:hi])
            tot = tot + gw_in[frm, :, lo:hi].astype(F32)
        return tot

    def terms(into, nb, lo, hi, own, others):
        acc = None
        parts = slice(4 * (nb % 2), 4 * (nb % 2) + 4)
        for yy in range(4):
            a = jnp.concatenate([into[yy, 1 - xl, :, lo:hi], into[yy, xl, :, lo:hi]], 0)
            rows = (nb // 2, parts)
            if yy:
                w = others[yy - 1, rows[0], rows[1], :, :, lo:hi].reshape(256, hi - lo)
            else:
                p, q = OWN[lo, hi]
                w = own[0, rows[0], rows[1], :, :, p:q].reshape(256, q - p)
            t = dot_nt(a, w)
            acc = t if acc is None else acc + t
        return acc

    gathered(a_keys, a_in, 0)
    go_keys = out_grad_send()
    for nb in range(4):
        acc = terms(a_in, nb, 0, 128, wa, wb)
        part_send[0, nb] = acc[:128].astype(BF16)
        part_own[0, :, 256 * nb:256 * nb + 256] = acc[128:]
    k_out = push(part_send.at[0], part_in.at[0], side)
    zc.step(1)
    weight_grad(0, 0)

    def backward_head(h, between=None):
        dk_t[...] = jnp.zeros_like(dk_t)

        def one(i, carry):
            rows = pl.ds(i * 512, 512)
            dpd = dot(ext[h, rows], v_t[h])
            ds = (p_all[h, rows].astype(F32) * dpd).astype(BF16)
            dq_t[:, rows] = dot(ds, kq[h]).T[:64]
            dk_t[...] += dot(kq_t[h, 64:128, rows], ds)
            return carry

        one(0, 0)
        got = between() if between else None
        one(1, 0)

        def maps(i, carry):
            rows = rows_of(i)
            d = jnp.stack([dk_t[:, rows] * (1.0 / LOG2E), dq_t[:, rows]])
            u = u_t[h, :, :, rows]
            d = r_t[h, :, :, rows] * (d - u * jnp.sum(u * d, 1, keepdims=True))
            gp[pl.ds(2 * i, 2), :, 128 + 128 * h:256 + 128 * h] = (
                d.reshape(128, 256).T.astype(BF16).reshape(2, 128, 128)
            )
            return carry

        lax.fori_loop(0, 4, maps, 0)
        return got

    backward_head(0)
    h0_keys = spread(gp, g_in, 128)
    zc.step(2)
    go_keys = out_grad_on(go_keys)
    weight_grad(128, 128)
    k_pair0 = pair_send(0, 256)

    def meanwhile():
        zc.step(3)
        return reduce_send(k_pair0, 0, 256)

    rs0 = backward_head(1, meanwhile)
    h1_keys = spread(gp, g_in, 256)
    zc.last()
    weight_grad(256, 384)
    out_grad(go_keys)
    k_pair1 = pair_send(256, 512)

    gathered(v_keys, g_in, 0)
    gathered(h0_keys, g_in, 128)
    zc.finish()
    for nb in range(4):
        held[nb] = terms(g_in, nb, 0, 256, wa, wc)
    rs1 = reduce_send(k_pair1, 256, 512)
    gathered(h1_keys, g_in, 256)
    back = []
    for nb in range(4):
        acc = held[nb] + terms(g_in, nb, 256, 384, wa, wc)
        part_send[1, nb] = acc[:128].astype(BF16)
        part_own[1, :, 256 * nb:256 * nb + 256] = acc[128:]
        back.append(push(part_send.at[1, nb], part_in.at[1, nb], side))

    def whole(which):
        return jnp.concatenate([part_in[which, nb] for nb in range(4)], -1).astype(F32)

    arrive(k_out, part_in.at[0])
    xf = xs[...]
    out_ref[0] = (xf + part_own[0] + whole(0)).reshape(32, 4, 1024).astype(BF16)
    got = reduce_done(rs0, 0, 256)
    gqkv_ref[2] = got[:, 0:128]
    got0 = got[:, 128:256]
    for nb in range(4):
        arrive(back[nb], part_in.at[1, nb])
    dn = (part_own[1] + whole(1)) * gain
    inner = jnp.mean(xf * dn, -1, keepdims=True)
    rs = lax.rsqrt(jnp.mean(xf * xf, -1, keepdims=True) + EPS)
    gt = g_two[xl].astype(F32) + rs * (dn - xf * (rs * rs * inner))
    gtok_ref[0] = gt.reshape(32, 4, 1024).astype(BF16)
    got1 = reduce_done(rs1, 256, 512)
    gout_ref[...] = got1[:, 0:128]
    got1 = got1[:, 128:256]
    gqkv_ref[0] = jnp.concatenate([got0[:, 64:], got1[:, 64:]], -1)
    gqkv_ref[1] = jnp.concatenate([got0[:, :64], got1[:, :64]], -1)
    for d in sends:
        d.wait_send()
    assert count[0] <= NSEM


def per_device(image_tokens, cotangent, noise_level, cond_table, head_scale, w_qkv, w_out):
    gain = lax.dynamic_slice_in_dim(cond_table, noise_level[0], 1, 0)
    vm = pl.BlockSpec(memory_space=pltpu.VMEM)
    sm = pl.BlockSpec(memory_space=pltpu.SMEM)
    V = pltpu.VMEM
    out, gtok, gqkv, gout = pl.pallas_call(
        kernel,
        out_shape=(
            jax.ShapeDtypeStruct((1, 32, 4, 1024), BF16),
            jax.ShapeDtypeStruct((1, 32, 4, 1024), BF16),
            jax.ShapeDtypeStruct((3, 32, 128), F32),
            jax.ShapeDtypeStruct((32, 128), F32),
        ),
        in_specs=[sm, vm, vm, vm, vm, vm],
        out_specs=[vm, vm, vm, vm],
        scratch_shapes=[
            V((128, 1024), F32),
            V((8, 2, 4, 16, 1024), BF16),
            V((2, 128, 1024), BF16),
            V((1024, 1024), BF16),
            V((1, 2, 8, 2, 32, 512), BF16),
            V((3, 2, 8, 2, 32, 128), BF16),
            V((3, 2, 8, 2, 32, 384), BF16),
            V((2, 2, 64, 1024), F32),
            V((2, 2, 1, 1024), F32),
            V((2, 128, 1024), BF16),
            V((2, 128, 1024), BF16),
            V((2, 1024, 128), BF16),
            V((2, 1024, 128), BF16),
            V((2, 128, 1024), BF16),
            V((2, 1024, 1024), BF16),
            V((8, 128, 128), BF16),
            V((2, 1024, 1), F32),
            V((2, 1024, 128), BF16),
            V((4, 2, 128, 128), BF16),
            V((8, 128, 128), BF16),
            V((4, 128, 1024), F32),
            V((3, 128, 1024), BF16),
            V((2, 64, 1024), BF16),
            V((2, 128, 1024), BF16),
            V((64, 1024), F32),
            V((64, 1024), F32),
            V((8, 128, 384), BF16),
            V((4, 2, 128, 128), BF16),
            V((4, 2, 128, 384), BF16),
            V((2, 128, 1024), F32),
            V((2, 4, 128, 256), BF16),
            V((2, 4, 128, 256), BF16),
            V((16, 2, 32, 512), F32),
            V((16, 2, 32, 512), BF16),
            V((16, 32, 512), BF16),
            V((16, 32, 512), BF16),
            V((16, 32, 512), BF16),
            V((4, 256, 256), F32),
            pltpu.SemaphoreType.DMA((NSEM,)),
            pltpu.SemaphoreType.DMA((NSEM,)),
        ],
        compiler_params=pltpu.CompilerParams(
            collective_id=0, has_side_effects=True, vmem_limit_bytes=56 * 1024 * 1024
        ),
        cost_estimate=pl.CostEstimate(
            flops=4_800_000_000, bytes_accessed=4_000_000, transcendentals=2_200_000
        ),
    )(head_scale, image_tokens, cotangent, gain, w_qkv, w_out.T)
    return out, gtok, gqkv, gout.T


def solution(mesh):
    return jax.shard_map(
        per_device,
        mesh=mesh,
        in_specs=(
            P("rows", None, "cols", None),
            P("rows", None, "cols", None),
            P("rows"),
            P(),
            P(),
            P(None, "rows", "cols"),
            P("cols", "rows"),
        ),
        out_specs=(
            P("rows", None, "cols", None),
            P("rows", None, "cols", None),
            P(None, "rows", "cols"),
            P("cols", "rows"),
        ),
        check_vma=False,
    )
```

```python
import jax
import jax.numpy as jnp
from jax import lax
from jax.experimental import pallas as pl
from jax.experimental.pallas import tpu as pltpu
from jax.sharding import PartitionSpec as P

EPS = 1e-06
LOG2E = 1.4426950408889634
MESH = pl.DeviceIdType.MESH
F32 = jnp.float32
BF16 = jnp.bfloat16
NSEM = 180
OWN = {(0, 128): (256, 384), (0, 256): (0, 256), (256, 384): (384, 512)}


def dot(a, b):
    return jnp.dot(a, b, preferred_element_type=F32)


def dot_nt(a, b):
    return lax.dot_general(a, b, (((1,), (1,)), ((), ())), preferred_element_type=F32)


def kernel(
    lvl_ref, hs_ref, x_hbm, g_hbm, cond_hbm, wqkv_ref, wout_ref,
    out_ref, gtok_ref, gqkv_ref, gout_ref,
    xs, n_all, g_two, n_t, wa, wb, wc,
    u_t, r_t, kq_t, kz, kq, v_x, v_t, p_all, attn, inv, ext, da_send, da_in,
    g_t, go_f, go_b, go_sib, go_send, go_half, go_in,
    dk_t, dq_t, gp, a_in, g_in, part_own, part_send, part_in,
    gw_f, gw_b, gw_sib, gw_sum, gw_in, held,
    x_ref, g_ref, cond_ref, send_sem, recv_sem, in_sem,
):
    r = lax.axis_index("rows")
    c = lax.axis_index("cols")
    y, xl = c // 2, c % 2
    xh, z, core = r // 16, (r // 2) % 8, r % 2
    m16 = r // 2

    def at_cols(yy, xx):
        return {"rows": r, "cols": yy * 2 + xx}

    def at_rows(xx, zz, cc):
        return {"rows": (xx * 8 + zz) * 2 + cc, "cols": c}

    yp, ym, yf = (y + 1) % 4, (y + 3) % 4, (y + 2) % 4
    up, down, side = at_cols(yp, xl), at_cols(ym, xl), at_cols(y, 1 - xl)
    zup, zdown = at_rows(xh, (z + 1) % 8, core), at_rows(xh, (z + 7) % 8, core)
    sib, over = at_rows(xh, z, 1 - core), at_rows(1 - xh, z, core)

    sends = []
    count = [0]

    def copy_of(k, src, dst, dev):
        return pltpu.make_async_remote_copy(
            src_ref=src, dst_ref=dst, send_sem=send_sem.at[k], recv_sem=recv_sem.at[k],
            device_id=dev, device_id_type=MESH,
        )

    def push(src, dst, dev):
        k = count[0]
        count[0] += 1
        d = copy_of(k, src, dst, dev)
        d.start()
        sends.append(d)
        return k

    def send(ref, dev):
        return push(ref, ref, dev)

    def arrive(k, ref):
        copy_of(k, ref, ref, side).wait_recv()

    barrier = pltpu.get_barrier_semaphore()
    peers = [at_cols((y + i) % 4, xl) for i in (1, 2, 3)]
    peers += [side, sib]
    peers += [{"rows": ((m16 + i) % 16) * 2 + core, "cols": c} for i in range(1, 16)]
    for dev in peers:
        pl.semaphore_signal(barrier, inc=1, device_id=dev, device_id_type=MESH)

    fetch = [
        pltpu.make_async_copy(src, dst, in_sem.at[i])
        for i, (src, dst) in enumerate(
            [(x_hbm.at[0], x_ref), (g_hbm.at[0], g_ref), (cond_hbm, cond_ref)]
        )
    ]
    for f in fetch:
        f.start()
    wq, wk = wqkv_ref[0], wqkv_ref[1]
    wa[0, xh, z, core] = jnp.concatenate(
        [wqkv_ref[2], wk[:, :64], wq[:, :64], wout_ref[...], wk[:, 64:], wq[:, 64:]], -1
    )
    kz[...] = jnp.zeros_like(kz)
    fetch[0].wait()
    xf = x_ref[...].astype(F32).reshape(128, 1024)
    xs[...] = xf
    rs = lax.rsqrt(jnp.mean(xf * xf, -1, keepdims=True) + EPS)
    fetch[2].wait()
    gain = cond_ref[pl.ds(lvl_ref[0], 1), :]
    n_all[c] = (xf * rs * gain).astype(BF16).reshape(2, 4, 16, 1024)
    fetch[1].wait()
    g_two[xl] = g_ref[...].astype(F32).reshape(128, 1024).astype(BF16)
    pl.semaphore_wait(barrier, len(peers))

    k_over = send(wa.at[0, xh, z, core], over)

    def to_rows(buf, x_from, other, pieces):
        keys = []
        for i in (1, 2, 3):
            for src, dst in pieces:
                k = push(
                    wa.at[0, x_from, z, core, :, src[0]:src[1]],
                    buf.at[3 - i, x_from, z, core, :, dst[0]:dst[1]],
                    at_cols((y + i) % 4, xl),
                )
                keys.append((k, buf.at[3 - i, (xh + other) % 2, z, core, :, dst[0]:dst[1]]))
        return keys

    def come(keys):
        for k, ref in keys:
            arrive(k, ref)

    out_piece = [((256, 384), (0, 128))]
    qkv_pieces = [((0, 256), (0, 256)), ((384, 512), (256, 384))]
    b_keys = to_rows(wb, xh, 0, out_piece)

    def slot(yy, xx):
        return yy * 2 + xx

    def stage_two(buf, ks):
        k_side, k_up, k_down = ks
        below, above, next_to = slot(ym, xl), slot(yp, xl), slot(y, 1 - xl)
        arrive(k_up, buf.at[below])
        b0 = send(buf.at[below, 0], up)
        b1 = send(buf.at[below, :, 3], side)
        arrive(k_down, buf.at[above])
        a0 = send(buf.at[above, 1], down)
        a1 = send(buf.at[above, :, 3], side)
        arrive(k_side, buf.at[next_to])
        s0 = send(buf.at[next_to, :, 0:3], up)
        s1 = send(buf.at[next_to, :, 0:3], down)
        return b0, b1, a0, a1, s0, s1

    def stage_three(buf, ks):
        b0, b1, a0, a1, s0, s1 = ks
        far, below, above = slot(yf, xl), slot(ym, 1 - xl), slot(yp, 1 - xl)
        arrive(b0, buf.at[far, 0])
        f0 = send(buf.at[far, 0, 3], side)
        arrive(a0, buf.at[far, 1])
        f1 = send(buf.at[far, 1, 3], side)
        arrive(s0, buf.at[below, :, 0:3])
        e0 = send(buf.at[below, 0, 0:3], up)
        arrive(s1, buf.at[above, :, 0:3])
        e1 = send(buf.at[above, 1, 0:3], down)
        return b1, a1, f0, f1, e0, e1

    def near_done(buf, ks):
        arrive(ks[0], buf.at[slot(ym, 1 - xl), :, 3])
        arrive(ks[1], buf.at[slot(yp, 1 - xl), :, 3])

    def far_done(buf, ks):
        f0, f1, e0, e1 = ks[2:]
        far = slot(yf, 1 - xl)
        arrive(e0, buf.at[far, 0, 0:3])
        arrive(e1, buf.at[far, 1, 0:3])
        arrive(f0, buf.at[far, 0, 3])
        arrive(f1, buf.at[far, 1, 3])

    def turned(yy):
        def one(j, carry):
            s = 2 * yy + j
            n_t[:, pl.ds(pl.multiple_of(s * 128, 128), 128)] = n_all[s].reshape(128, 1024).T
            return carry
        lax.fori_loop(0, 2, one, 0)

    n_own = n_all.at[c]
    n_keys = send(n_own, side), send(n_own, up), send(n_own, down)

    class OverZ:
        def __init__(self, buf):
            self.buf = buf
            own = self.block(0)
            self.near = [send(own, self.to(d)) for d in (2, -2, 1, -1)]

        def to(self, d):
            return at_rows(xh, (z + 8 + d) % 8, core)

        def block(self, d):
            return self.buf.at[:, :, (z + 8 + d) % 8, core]

        def half(self, d, h):
            return self.buf.at[:, h, (z + 8 + d) % 8, core]

        def forward(self):
            self.far = []
            for k, d, h in ((self.near[0], -2, 0), (self.near[1], 2, 1)):
                arrive(k, self.block(d))
                one = 1 if d < 0 else -1
                self.far.append(send(self.block(d), self.to(one)))
                self.far.append(send(self.half(d, h), self.to(2 * one)))

        def to_sib(self):
            arrive(self.near[2], self.block(-1))
            arrive(self.near[3], self.block(1))
            arrive(self.far[0], self.block(-3))
            arrive(self.far[2], self.block(3))
            arrive(self.far[1], self.half(4, 0))
            arrive(self.far[3], self.half(4, 1))
            self.k_sib = send(self.buf.at[:, :, :, core], sib)

        def finish(self):
            arrive(self.k_sib, self.buf.at[:, :, :, 1 - core])

    class Ring:
        def __init__(self, buf):
            self.buf = buf
            self.sib_keys = []
            self.up, self.down = send(self.block(z), zup), send(self.block(z), zdown)
            self.to_sib(z)

        def block(self, zz):
            return self.buf.at[:, :, zz, core]

        def half(self, zz, h):
            return self.buf.at[:, h, zz, core]

        def to_sib(self, zz):
            self.sib_keys.append((send(self.block(zz), sib), zz))

        def step(self, d):
            lo, hi = (z + 8 - d) % 8, (z + d) % 8
            arrive(self.up, self.block(lo))
            self.up = send(self.block(lo) if d < 3 else self.half(lo, 0), zup)
            self.to_sib(lo)
            arrive(self.down, self.block(hi))
            self.down = send(self.block(hi) if d < 3 else self.half(hi, 1), zdown)
            self.to_sib(hi)

        def last(self):
            opp = (z + 4) % 8
            arrive(self.up, self.half(opp, 0))
            arrive(self.down, self.half(opp, 1))
            self.to_sib(opp)

        def finish(self):
            for k, zz in self.sib_keys:
                arrive(k, self.buf.at[:, :, zz, 1 - core])

    arrive(k_over, wa.at[0, 1 - xh, z, core])
    za = OverZ(wa)
    b_keys += to_rows(wb, 1 - xh, 1, out_piece)
    za.forward()
    come(b_keys)
    zb = OverZ(wb)
    n_keys = stage_two(n_all, n_keys)
    k_g = send(g_two.at[xl], side)
    za.to_sib()
    zb.forward()
    turned(y)
    n_keys = stage_three(n_all, n_keys)
    za.finish()

    sc = [hs_ref[c * 2], hs_ref[c * 2 + 1]]
    lane = lax.broadcasted_iota(jnp.int32, (256, 128), 1)
    first = lane < 64
    ones = [
        jnp.where((lane == 64) | (lane == 65), 1.0, 0.0),
        jnp.where(lane < 2, 1.0, 0.0),
    ]

    def rows_of(i):
        return pl.ds(pl.multiple_of(i * 256, 256), 256)

    def project(i):
        rows = rows_of(i)
        n = n_all[pl.ds(2 * i, 2)].reshape(256, 1024)
        w = wa[0].reshape(1024, 512)
        res = dot(n, jnp.concatenate([w[:, :256], w[:, 384:]], -1))
        vv = res[:, :128]
        for h in (0, 1):
            t = res[:, 128 + 128 * h:256 + 128 * h].T.reshape(2, 64, 256)
            rn = lax.rsqrt(jnp.sum(t * t, 1, keepdims=True) + EPS)
            t = t * rn
            u_t[h, :, :, rows] = t
            r_t[h, 0, :, rows] = rn[0]
            r_t[h, 1, :, rows] = rn[1] * sc[h]
            both = jnp.concatenate([t[0], t[1] * (sc[h] * LOG2E)], 0)
            kq_t[h, :, rows] = both.astype(BF16)
            kz[h, 64:128, rows] = t[0].astype(BF16)
            kq[h, rows] = both.T.astype(BF16)
            vx = jnp.where(first if h == 0 else ~first, vv, ones[h]).astype(BF16)
            v_x[h, rows] = vx
            v_t[h, :, rows] = vx.T

    def project_near(j, carry):
        yy = (y + 1 + 2 * j) % 4
        project(yy)
        turned(yy)
        return carry

    project(y)
    near_done(n_all, n_keys)
    c_keys = to_rows(wc, xh, 0, qkv_pieces) + to_rows(wc, 1 - xh, 1, qkv_pieces)
    zb.to_sib()
    lax.fori_loop(0, 2, project_near, 0)
    far_done(n_all, n_keys)
    project(yf)

    zb.finish()
    arrive(k_g, g_two.at[1 - xl])
    gg = g_two[...].reshape(256, 1024)
    g_t[...] = gg.T
    for a in (0, 2):
        w0 = wa[0, :, :, :, :, 256:384] if a == 0 else wb[a - 1]
        w = jnp.concatenate([w0.reshape(1024, 128), wb[a].reshape(1024, 128)], -1)
        t = dot(gg, w).astype(BF16)
        da_send[a] = t[:, :128].reshape(2, 128, 128)
        da_send[a + 1] = t[:, 128:].reshape(2, 128, 128)
    da_keys = []
    for i in (1, 2, 3):
        dst = da_in.at[pl.ds(2 * y, 2)]
        da_keys.append((push(da_send.at[i], dst, at_cols((y + i) % 4, xl)), (y + 4 - i) % 4))
    da_in[pl.ds(2 * y, 2)] = da_send[0]
    come(c_keys)
    zc = Ring(wc)

    lane5 = lax.broadcasted_iota(jnp.int32, (512, 128), 1)

    def forward(i):
        rows = pl.ds(i * 512, 512)
        outs = []
        for h in (0, 1):
            s = dot(kq[h, rows], kz[h])
            p = jnp.exp2(s).astype(BF16)
            p_all[h, rows] = p
            num = dot(p, v_x[h])
            den = num[:, 64:65] if h == 0 else num[:, 0:1]
            iv = (1.0 / den).astype(BF16).astype(F32)
            inv[h, rows] = iv
            outs.append(num * iv)
        attn[pl.ds(4 * i, 4)] = jnp.where(lane5 < 64, outs[0], outs[1]).astype(BF16).reshape(
            4, 128, 128
        )

    forward(0)
    forward(1)

    def spread(buf, into, lo):
        keys = []
        lanes = slice(lo, lo + 128)
        for i in (2, 1, 3):
            to = (y + i) % 4
            src = buf.at[pl.ds(2 * to, 2), :, lanes]
            keys.append((push(src, into.at[4 - i, :, :, lanes], at_cols(to, xl)), 4 - i))
        into[0, :, :, lanes] = buf[pl.ds(2 * y, 2), :, lanes]
        return keys

    def gathered(keys, into, lo):
        for k, rel in keys:
            arrive(k, into.at[rel, :, :, lo:lo + 128])

    a_keys = spread(attn, a_in, 0)
    zc.step(1)
    turned(yf)

    for k, frm in da_keys:
        arrive(k, da_in.at[pl.ds(2 * frm, 2)])

    def cot(i, carry):
        rows = rows_of(i)
        dd = da_in[pl.ds(2 * i, 2)].reshape(256, 128).astype(F32)
        prod = dd * attn[pl.ds(2 * i, 2)].reshape(256, 128).astype(F32)
        for h in (0, 1):
            iv = inv[h, rows]
            mine = first if h == 0 else ~first
            delta = jnp.sum(jnp.where(mine, prod, 0.0), -1, keepdims=True) * iv
            hi = delta.astype(BF16).astype(F32)
            lo = delta - hi
            at = 64 if h == 0 else 0
            e = jnp.where(mine, dd * iv, jnp.where(lane == at, -hi, jnp.where(lane == at + 1, -lo, 0.0)))
            ext[h, rows] = e.astype(BF16)
        return carry

    lax.fori_loop(0, 4, cot, 0)
    dvs = []
    for h in (0, 1):
        e_t = ext[h].T
        dvs.append(dot(e_t[64 * h:64 * h + 64], p_all[h]))
    gp[:, :, 0:128] = jnp.concatenate(dvs, 0).T.astype(BF16).reshape(8, 128, 128)
    v_keys = spread(gp, g_in, 0)
    zc.step(2)

    def weight_grad(lo, to):
        res = dot(n_t[...], gp[:, :, lo:lo + 128].reshape(1024, 128))
        gw_f[:, :, :, to:to + 128] = res.reshape(16, 2, 32, 128)
        gw_b[:, :, :, to:to + 128] = res.astype(BF16).reshape(16, 2, 32, 128)

    def out_grad_send():
        for i in range(4):
            go = dot(g_t[...], a_in[i].reshape(256, 128)).reshape(16, 2, 32, 128)
            go_f[i] = go
            go_b[i] = go.astype(BF16)
        return push(go_b.at[:, :, 1 - core], go_sib, sib)

    def out_far_send(k):
        arrive(k, go_sib)
        for i in range(4):
            go_f[i, :, core] = go_f[i, :, core] + go_sib[i].astype(F32)
        go_send[2] = go_f[2, :, core].astype(BF16)
        return (
            push(go_send.at[2, 0:8], go_half.at[0], up),
            push(go_send.at[2, 8:16], go_half.at[1], down),
        )

    def out_grad_on(keys):
        arrive(keys[0], go_half.at[0])
        arrive(keys[1], go_half.at[1])
        go_send[0, 0:8] = (go_f[1, 0:8, core] + go_half[0].astype(F32)).astype(BF16)
        go_send[0, 8:16] = go_f[1, 8:16, core].astype(BF16)
        go_send[1, 0:8] = go_f[3, 0:8, core].astype(BF16)
        go_send[1, 8:16] = (go_f[3, 8:16, core] + go_half[1].astype(F32)).astype(BF16)
        return push(go_send.at[0], go_in.at[0], up), push(go_send.at[1], go_in.at[1], down)

    def out_grad(keys):
        arrive(keys[0], go_in.at[0])
        arrive(keys[1], go_in.at[1])
        tot = go_f[0, :, core] + go_in[0].astype(F32) + go_in[1].astype(F32)
        gw_f[:, core, :, 256:384] = tot
        gw_sum[:, :, 256:384] = tot.astype(BF16)

    def pair_send(lo, hi):
        return push(gw_b.at[:, 1 - core, :, lo:hi], gw_sib.at[:, :, lo:hi], sib)

    def reduce_send(k, lo, hi, start):
        arrive(k, gw_sib.at[:, :, lo:hi])
        tot = gw_f[:, core, :, lo:hi] + gw_sib[:, :, lo:hi].astype(F32)
        gw_f[:, core, :, lo:hi] = tot
        gw_sum[:, :, lo:hi] = tot.astype(BF16)
        keys = []
        for dz in (4, 3, 5, 2, 6, 1, 7, 0):
            for dx in (1, 0):
                if dx or dz:
                    to = ((xh + dx) % 2) * 8 + (z + dz) % 8
                    frm = ((xh + dx) % 2) * 8 + (z + 8 - dz) % 8
                    dev = {"rows": to * 2 + core, "cols": c}
                    keys.append(
                        (push(gw_sum.at[to, :, start:hi], gw_in.at[m16, :, start:hi], dev), frm)
                    )
        return keys

    def reduce_done(keys, lo, hi):
        tot = gw_f[m16, core, :, lo:hi]
        for k, frm in keys:
            arrive(k, gw_in.at[frm, :, lo:hi])
            tot = tot + gw_in[frm, :, lo:hi].astype(F32)
        return tot

    def terms(into, nb, lo, hi, own, others):
        acc = None
        parts = slice(4 * (nb % 2), 4 * (nb % 2) + 4)
        for yy in range(4):
            a = jnp.concatenate([into[yy, 1 - xl, :, lo:hi], into[yy, xl, :, lo:hi]], 0)
            rows = (nb // 2, parts)
            if yy:
                w = others[yy - 1, rows[0], rows[1], :, :, lo:hi].reshape(256, hi - lo)
            else:
                p, q = OWN[lo, hi]
                w = own[0, rows[0], rows[1], :, :, p:q].reshape(256, q - p)
            t = dot_nt(a, w)
            acc = t if acc is None else acc + t
        return acc

    gathered(a_keys, a_in, 0)
    k_go = out_grad_send()
    for nb in range(4):
        acc = terms(a_in, nb, 0, 128, wa, wb)
        part_send[0, nb] = acc[:128].astype(BF16)
        part_own[0, :, 256 * nb:256 * nb + 256] = acc[128:]
    k_out = push(part_send.at[0], part_in.at[0], side)
    go_keys = out_far_send(k_go)
    weight_grad(0, 0)
    zc.step(3)

    def backward_head(h, between=None):
        dk_t[...] = jnp.zeros_like(dk_t)

        def one(i, carry):
            rows = pl.ds(i * 512, 512)
            dpd = dot(ext[h, rows], v_t[h])
            ds = (p_all[h, rows].astype(F32) * dpd).astype(BF16)
            dq_t[:, rows] = dot(ds, kq[h]).T[:64]
            dk_t[...] += dot(kq_t[h, 64:128, rows], ds)
            return carry

        one(0, 0)
        got = between() if between else None
        one(1, 0)

        def maps(i, carry):
            rows = rows_of(i)
            d = jnp.stack([dk_t[:, rows] * (1.0 / LOG2E), dq_t[:, rows]])
            u = u_t[h, :, :, rows]
            d = r_t[h, :, :, rows] * (d - u * jnp.sum(u * d, 1, keepdims=True))
            gp[pl.ds(2 * i, 2), :, 128 + 128 * h:256 + 128 * h] = (
                d.reshape(128, 256).T.astype(BF16).reshape(2, 128, 128)
            )
            return carry

        lax.fori_loop(0, 4, maps, 0)
        return got

    go_keys = backward_head(0, lambda: out_grad_on(go_keys))
    h0_keys = spread(gp, g_in, 128)
    zc.last()
    weight_grad(128, 128)
    k_pair0 = pair_send(0, 256)

    def meanwhile():
        return reduce_send(k_pair0, 0, 256, 0)

    rs0 = backward_head(1, meanwhile)
    h1_keys = spread(gp, g_in, 256)
    weight_grad(256, 384)
    k_pair1 = pair_send(384, 512)
    out_grad(go_keys)

    gathered(v_keys, g_in, 0)
    gathered(h0_keys, g_in, 128)
    zc.finish()
    for nb in range(4):
        held[nb] = terms(g_in, nb, 0, 256, wa, wc)
    rs1 = reduce_send(k_pair1, 384, 512, 256)
    gathered(h1_keys, g_in, 256)
    back = []
    for nb in range(4):
        acc = held[nb] + terms(g_in, nb, 256, 384, wa, wc)
        part_send[1, nb] = acc[:128].astype(BF16)
        part_own[1, :, 256 * nb:256 * nb + 256] = acc[128:]
        back.append(push(part_send.at[1, nb], part_in.at[1, nb], side))

    def whole(which):
        return jnp.concatenate([part_in[which, nb] for nb in range(4)], -1).astype(F32)

    arrive(k_out, part_in.at[0])
    xf = xs[...]
    out_ref[0] = (xf + part_own[0] + whole(0)).reshape(32, 4, 1024).astype(BF16)
    got = reduce_done(rs0, 0, 256)
    gqkv_ref[2] = got[:, 0:128]
    got0 = got[:, 128:256]
    for nb in range(4):
        arrive(back[nb], part_in.at[1, nb])
    dn = (part_own[1] + whole(1)) * gain
    inner = jnp.mean(xf * dn, -1, keepdims=True)
    rs = lax.rsqrt(jnp.mean(xf * xf, -1, keepdims=True) + EPS)
    gt = g_two[xl].astype(F32) + rs * (dn - xf * (rs * rs * inner))
    gtok_ref[0] = gt.reshape(32, 4, 1024).astype(BF16)
    got1 = reduce_done(rs1, 256, 512)
    gout_ref[...] = got1[:, 0:128]
    got1 = got1[:, 128:256]
    gqkv_ref[0] = jnp.concatenate([got0[:, 64:], got1[:, 64:]], -1)
    gqkv_ref[1] = jnp.concatenate([got0[:, :64], got1[:, :64]], -1)
    for d in sends:
        d.wait_send()
    assert count[0] <= NSEM


def hand_on(*refs):
    for src, dst in zip(refs[:4], refs[4:]):
        dst[...] = src[...]


def per_device(image_tokens, cotangent, noise_level, cond_table, head_scale, w_qkv, w_out):
    hbm = pl.BlockSpec(memory_space=pl.ANY)
    vm = pl.BlockSpec(memory_space=pltpu.VMEM)
    sm = pl.BlockSpec(memory_space=pltpu.SMEM)
    V = pltpu.VMEM
    out, gtok, gqkv, gout = pl.pallas_call(
        kernel,
        out_shape=(
            jax.ShapeDtypeStruct((1, 32, 4, 1024), BF16),
            jax.ShapeDtypeStruct((1, 32, 4, 1024), BF16),
            jax.ShapeDtypeStruct((3, 32, 128), F32),
            jax.ShapeDtypeStruct((32, 128), F32),
        ),
        in_specs=[sm, sm, hbm, hbm, hbm, vm, vm],
        out_specs=[vm, vm, vm, vm],
        scratch_shapes=[
            V((128, 1024), F32),
            V((8, 2, 4, 16, 1024), BF16),
            V((2, 128, 1024), BF16),
            V((1024, 1024), BF16),
            V((1, 2, 8, 2, 32, 512), BF16),
            V((3, 2, 8, 2, 32, 128), BF16),
            V((3, 2, 8, 2, 32, 384), BF16),
            V((2, 2, 64, 1024), F32),
            V((2, 2, 1, 1024), F32),
            V((2, 128, 1024), BF16),
            V((2, 128, 1024), BF16),
            V((2, 1024, 128), BF16),
            V((2, 1024, 128), BF16),
            V((2, 128, 1024), BF16),
            V((2, 1024, 1024), BF16),
            V((8, 128, 128), BF16),
            V((2, 1024, 1), F32),
            V((2, 1024, 128), BF16),
            V((4, 2, 128, 128), BF16),
            V((8, 128, 128), BF16),
            V((1024, 256), BF16),
            V((4, 16, 2, 32, 128), F32),
            V((4, 16, 2, 32, 128), BF16),
            V((4, 16, 32, 128), BF16),
            V((3, 16, 32, 128), BF16),
            V((2, 8, 32, 128), BF16),
            V((2, 16, 32, 128), BF16),
            V((64, 1024), F32),
            V((64, 1024), F32),
            V((8, 128, 384), BF16),
            V((4, 2, 128, 128), BF16),
            V((4, 2, 128, 384), BF16),
            V((2, 128, 1024), F32),
            V((2, 4, 128, 256), BF16),
            V((2, 4, 128, 256), BF16),
            V((16, 2, 32, 512), F32),
            V((16, 2, 32, 512), BF16),
            V((16, 32, 512), BF16),
            V((16, 32, 512), BF16),
            V((16, 32, 512), BF16),
            V((4, 256, 256), F32),
            V((32, 4, 1024), BF16),
            V((32, 4, 1024), BF16),
            V((256, 1024), F32),
            pltpu.SemaphoreType.DMA((NSEM,)),
            pltpu.SemaphoreType.DMA((NSEM,)),
            pltpu.SemaphoreType.DMA((3,)),
        ],
        compiler_params=pltpu.CompilerParams(
            collective_id=0, has_side_effects=True, vmem_limit_bytes=56 * 1024 * 1024
        ),
        cost_estimate=pl.CostEstimate(
            flops=4_800_000_000, bytes_accessed=4_000_000, transcendentals=2_200_000
        ),
    )(noise_level, head_scale, image_tokens, cotangent, cond_table, w_qkv, w_out.T)
    got = (out, gtok, gqkv, gout)
    out, gtok, gqkv, gout = pl.pallas_call(
        hand_on,
        out_shape=tuple(jax.ShapeDtypeStruct(a.shape, a.dtype) for a in got),
        in_specs=[vm] * 4,
        out_specs=[vm] * 4,
    )(*got)
    return out, gtok, gqkv, gout.T


def solution(mesh):
    return jax.shard_map(
        per_device,
        mesh=mesh,
        in_specs=(
            P("rows", None, "cols", None),
            P("rows", None, "cols", None),
            P("rows"),
            P(),
            P(),
            P(None, "rows", "cols"),
            P("cols", "rows"),
        ),
        out_specs=(
            P("rows", None, "cols", None),
            P("rows", None, "cols", None),
            P(None, "rows", "cols"),
            P("cols", "rows"),
        ),
        check_vma=False,
    )
```

```python
import jax
import jax.numpy as jnp
from jax import lax
from jax.experimental import pallas as pl
from jax.experimental.pallas import tpu as pltpu
from jax.sharding import PartitionSpec as P

EPS = 1e-06
LOG2E = 1.4426950408889634
MESH = pl.DeviceIdType.MESH
F32 = jnp.float32
BF16 = jnp.bfloat16
NSEM = 180
OWN = {(0, 128): (256, 384), (0, 256): (0, 256), (256, 384): (384, 512)}


def dot(a, b):
    return jnp.dot(a, b, preferred_element_type=F32)


def kernel(
    lvl_ref, hs_ref, x_hbm, g_hbm, cond_hbm, wqkv_ref, wout_ref,
    out_ref, gtok_ref, gqkv_ref, gout_ref,
    xs, n_all, g_two, n_t, wa, wb, wc,
    u_t, r_t, kq_t, kz, kq, v_x, v_t, p_all, attn, inv, ext, da_send, da_in,
    g_t, go_f, go_b, go_sib, go_send, go_half, go_in,
    dk_t, dq_t, gp, a_in, g_in, part_own, part_send, part_in,
    gw_f, gw_b, gw_sib, gw_sum, gw_in, held,
    x_ref, g_ref, cond_ref, send_sem, recv_sem, in_sem,
):
    r = lax.axis_index("rows")
    c = lax.axis_index("cols")
    y, xl = c // 2, c % 2
    xh, z, core = r // 16, (r // 2) % 8, r % 2
    m16 = r // 2

    def at_cols(yy, xx):
        return {"rows": r, "cols": yy * 2 + xx}

    def at_rows(xx, zz, cc):
        return {"rows": (xx * 8 + zz) * 2 + cc, "cols": c}

    yp, ym, yf = (y + 1) % 4, (y + 3) % 4, (y + 2) % 4
    up, down, side = at_cols(yp, xl), at_cols(ym, xl), at_cols(y, 1 - xl)
    zup, zdown = at_rows(xh, (z + 1) % 8, core), at_rows(xh, (z + 7) % 8, core)
    sib, over = at_rows(xh, z, 1 - core), at_rows(1 - xh, z, core)

    sends = []
    count = [0]

    def copy_of(k, src, dst, dev):
        return pltpu.make_async_remote_copy(
            src_ref=src, dst_ref=dst, send_sem=send_sem.at[k], recv_sem=recv_sem.at[k],
            device_id=dev, device_id_type=MESH,
        )

    def push(src, dst, dev):
        k = count[0]
        count[0] += 1
        d = copy_of(k, src, dst, dev)
        d.start()
        sends.append(d)
        return k

    def send(ref, dev):
        return push(ref, ref, dev)

    def arrive(k, ref):
        copy_of(k, ref, ref, side).wait_recv()

    barrier = pltpu.get_barrier_semaphore()
    peers = [at_cols((y + i) % 4, xl) for i in (1, 2, 3)]
    peers += [side, sib]
    peers += [{"rows": ((m16 + i) % 16) * 2 + core, "cols": c} for i in range(1, 16)]
    for dev in peers:
        pl.semaphore_signal(barrier, inc=1, device_id=dev, device_id_type=MESH)

    fetch = [
        pltpu.make_async_copy(src, dst, in_sem.at[i])
        for i, (src, dst) in enumerate(
            [(x_hbm.at[0], x_ref), (g_hbm.at[0], g_ref), (cond_hbm, cond_ref)]
        )
    ]
    for f in fetch:
        f.start()
    wq, wk = wqkv_ref[0], wqkv_ref[1]
    wa[0, xh, z, core] = jnp.concatenate(
        [wqkv_ref[2], wk[:, :64], wq[:, :64], wout_ref[...], wk[:, 64:], wq[:, 64:]], -1
    )
    kz[...] = jnp.zeros_like(kz)
    fetch[0].wait()
    xf = x_ref[...].astype(F32).reshape(128, 1024)
    xs[...] = xf
    rs = lax.rsqrt(jnp.mean(xf * xf, -1, keepdims=True) + EPS)
    fetch[2].wait()
    gain = cond_ref[pl.ds(lvl_ref[0], 1), :]
    n_all[c] = (xf * rs * gain).astype(BF16).reshape(2, 4, 16, 1024)
    fetch[1].wait()
    g_two[xl] = g_ref[...].astype(F32).reshape(128, 1024).astype(BF16)
    pl.semaphore_wait(barrier, len(peers))

    k_over = send(wa.at[0, xh, z, core], over)

    def to_rows(buf, x_from, other, pieces):
        keys = []
        for i in (1, 2, 3):
            for src, dst in pieces:
                k = push(
                    wa.at[0, x_from, z, core, :, src[0]:src[1]],
                    buf.at[3 - i, x_from, z, core, :, dst[0]:dst[1]],
                    at_cols((y + i) % 4, xl),
                )
                keys.append((k, buf.at[3 - i, (xh + other) % 2, z, core, :, dst[0]:dst[1]]))
        return keys

    def come(keys):
        for k, ref in keys:
            arrive(k, ref)

    out_piece = [((256, 384), (0, 128))]
    qkv_pieces = [((0, 256), (0, 256)), ((384, 512), (256, 384))]
    b_keys = to_rows(wb, xh, 0, out_piece)

    def slot(yy, xx):
        return yy * 2 + xx

    def stage_two(buf, ks):
        k_side, k_up, k_down = ks
        below, above, next_to = slot(ym, xl), slot(yp, xl), slot(y, 1 - xl)
        arrive(k_up, buf.at[below])
        b0 = send(buf.at[below, 0], up)
        b1 = send(buf.at[below, :, 3], side)
        arrive(k_down, buf.at[above])
        a0 = send(buf.at[above, 1], down)
        a1 = send(buf.at[above, :, 3], side)
        arrive(k_side, buf.at[next_to])
        s0 = send(buf.at[next_to, :, 0:3], up)
        s1 = send(buf.at[next_to, :, 0:3], down)
        return b0, b1, a0, a1, s0, s1

    def stage_three(buf, ks):
        b0, b1, a0, a1, s0, s1 = ks
        far, below, above = slot(yf, xl), slot(ym, 1 - xl), slot(yp, 1 - xl)
        arrive(b0, buf.at[far, 0])
        f0 = send(buf.at[far, 0, 3], side)
        arrive(a0, buf.at[far, 1])
        f1 = send(buf.at[far, 1, 3], side)
        arrive(s0, buf.at[below, :, 0:3])
        e0 = send(buf.at[below, 0, 0:3], up)
        arrive(s1, buf.at[above, :, 0:3])
        e1 = send(buf.at[above, 1, 0:3], down)
        return b1, a1, f0, f1, e0, e1

    def near_done(buf, ks):
        arrive(ks[0], buf.at[slot(ym, 1 - xl), :, 3])
        arrive(ks[1], buf.at[slot(yp, 1 - xl), :, 3])

    def far_done(buf, ks):
        f0, f1, e0, e1 = ks[2:]
        far = slot(yf, 1 - xl)
        arrive(e0, buf.at[far, 0, 0:3])
        arrive(e1, buf.at[far, 1, 0:3])
        arrive(f0, buf.at[far, 0, 3])
        arrive(f1, buf.at[far, 1, 3])

    def turned(yy):
        def one(j, carry):
            s = 2 * yy + j
            n_t[:, pl.ds(pl.multiple_of(s * 128, 128), 128)] = n_all[s].reshape(128, 1024).T
            return carry
        lax.fori_loop(0, 2, one, 0)

    n_own = n_all.at[c]
    n_keys = send(n_own, side), send(n_own, up), send(n_own, down)

    class OverZ:
        def __init__(self, buf):
            self.buf = buf
            own = self.block(0)
            self.near = [send(own, self.to(d)) for d in (2, -2, 1, -1)]

        def to(self, d):
            return at_rows(xh, (z + 8 + d) % 8, core)

        def block(self, d):
            return self.buf.at[:, :, (z + 8 + d) % 8, core]

        def half(self, d, h):
            return self.buf.at[:, h, (z + 8 + d) % 8, core]

        def forward(self):
            self.far = []
            for k, d, h in ((self.near[0], -2, 0), (self.near[1], 2, 1)):
                arrive(k, self.block(d))
                one = 1 if d < 0 else -1
                self.far.append(send(self.block(d), self.to(one)))
                self.far.append(send(self.half(d, h), self.to(2 * one)))

        def to_sib(self):
            arrive(self.near[2], self.block(-1))
            arrive(self.near[3], self.block(1))
            arrive(self.far[0], self.block(-3))
            arrive(self.far[2], self.block(3))
            arrive(self.far[1], self.half(4, 0))
            arrive(self.far[3], self.half(4, 1))
            self.k_sib = send(self.buf.at[:, :, :, core], sib)

        def finish(self):
            arrive(self.k_sib, self.buf.at[:, :, :, 1 - core])

    class Ring:
        def __init__(self, buf):
            self.buf = buf
            self.sib_keys = []
            self.up, self.down = send(self.block(z), zup), send(self.block(z), zdown)
            self.to_sib(z)

        def block(self, zz):
            return self.buf.at[:, :, zz, core]

        def half(self, zz, h):
            return self.buf.at[:, h, zz, core]

        def to_sib(self, zz):
            self.sib_keys.append((send(self.block(zz), sib), zz))

        def step(self, d):
            lo, hi = (z + 8 - d) % 8, (z + d) % 8
            arrive(self.up, self.block(lo))
            self.up = send(self.block(lo) if d < 3 else self.half(lo, 0), zup)
            self.to_sib(lo)
            arrive(self.down, self.block(hi))
            self.down = send(self.block(hi) if d < 3 else self.half(hi, 1), zdown)
            self.to_sib(hi)

        def last(self):
            opp = (z + 4) % 8
            arrive(self.up, self.half(opp, 0))
            arrive(self.down, self.half(opp, 1))
            self.to_sib(opp)

        def finish(self):
            for k, zz in self.sib_keys:
                arrive(k, self.buf.at[:, :, zz, 1 - core])

    arrive(k_over, wa.at[0, 1 - xh, z, core])
    za = OverZ(wa)
    b_keys += to_rows(wb, 1 - xh, 1, out_piece)
    za.forward()
    come(b_keys)
    zb = OverZ(wb)
    n_keys = stage_two(n_all, n_keys)
    k_g = send(g_two.at[xl], side)
    za.to_sib()
    zb.forward()
    turned(y)
    n_keys = stage_three(n_all, n_keys)
    za.finish()

    sc = [hs_ref[c * 2], hs_ref[c * 2 + 1]]
    lane = lax.broadcasted_iota(jnp.int32, (256, 128), 1)
    first = lane < 64
    ones = [
        jnp.where((lane == 64) | (lane == 65), 1.0, 0.0),
        jnp.where(lane < 2, 1.0, 0.0),
    ]

    def rows_of(i):
        return pl.ds(pl.multiple_of(i * 256, 256), 256)

    def project(i):
        rows = rows_of(i)
        n = n_all[pl.ds(2 * i, 2)].reshape(256, 1024)
        w = wa[0].reshape(1024, 512)
        res = dot(n, jnp.concatenate([w[:, :256], w[:, 384:]], -1))
        vv = res[:, :128]
        for h in (0, 1):
            t = res[:, 128 + 128 * h:256 + 128 * h].T.reshape(2, 64, 256)
            rn = lax.rsqrt(jnp.sum(t * t, 1, keepdims=True) + EPS)
            t = t * rn
            u_t[h, :, :, rows] = t
            r_t[h, 0, :, rows] = rn[0]
            r_t[h, 1, :, rows] = rn[1] * sc[h]
            both = jnp.concatenate([t[0], t[1] * (sc[h] * LOG2E)], 0)
            kq_t[h, :, rows] = both.astype(BF16)
            kz[h, 64:128, rows] = t[0].astype(BF16)
            kq[h, rows] = both.T.astype(BF16)
            vx = jnp.where(first if h == 0 else ~first, vv, ones[h]).astype(BF16)
            v_x[h, rows] = vx
            v_t[h, :, rows] = vx.T

    def project_near(j, carry):
        yy = (y + 1 + 2 * j) % 4
        project(yy)
        turned(yy)
        return carry

    project(y)
    near_done(n_all, n_keys)
    c_keys = to_rows(wc, xh, 0, qkv_pieces) + to_rows(wc, 1 - xh, 1, qkv_pieces)
    zb.to_sib()
    lax.fori_loop(0, 2, project_near, 0)
    far_done(n_all, n_keys)
    project(yf)

    zb.finish()
    arrive(k_g, g_two.at[1 - xl])
    gg = g_two[...].reshape(256, 1024)
    g_t[...] = gg.T
    for a in (0, 2):
        w0 = wa[0, :, :, :, :, 256:384] if a == 0 else wb[a - 1]
        w = jnp.concatenate([w0.reshape(1024, 128), wb[a].reshape(1024, 128)], -1)
        t = dot(gg, w).astype(BF16)
        da_send[a] = t[:, :128].reshape(2, 128, 128)
        da_send[a + 1] = t[:, 128:].reshape(2, 128, 128)
    da_keys = []
    for i in (1, 2, 3):
        dst = da_in.at[pl.ds(2 * y, 2)]
        da_keys.append((push(da_send.at[i], dst, at_cols((y + i) % 4, xl)), (y + 4 - i) % 4))
    da_in[pl.ds(2 * y, 2)] = da_send[0]
    come(c_keys)
    zc = Ring(wc)

    lane5 = lax.broadcasted_iota(jnp.int32, (512, 128), 1)

    def forward(i):
        rows = pl.ds(i * 512, 512)
        outs = []
        for h in (0, 1):
            s = dot(kq[h, rows], kz[h])
            p = jnp.exp2(s).astype(BF16)
            p_all[h, rows] = p
            num = dot(p, v_x[h])
            den = num[:, 64:65] if h == 0 else num[:, 0:1]
            iv = (1.0 / den).astype(BF16).astype(F32)
            inv[h, rows] = iv
            outs.append(num * iv)
        attn[pl.ds(4 * i, 4)] = jnp.where(lane5 < 64, outs[0], outs[1]).astype(BF16).reshape(
            4, 128, 128
        )

    forward(0)
    forward(1)

    def spread(buf, into, lo):
        keys = []
        lanes = slice(lo, lo + 128)
        for i in (2, 1, 3):
            to = (y + i) % 4
            src = buf.at[pl.ds(2 * to, 2), :, lanes]
            keys.append((push(src, into.at[4 - i, :, :, lanes], at_cols(to, xl)), 4 - i))
        into[0, :, :, lanes] = buf[pl.ds(2 * y, 2), :, lanes]
        return keys

    def gathered(keys, into, lo):
        for k, rel in keys:
            arrive(k, into.at[rel, :, :, lo:lo + 128])

    a_keys = spread(attn, a_in, 0)
    zc.step(1)
    turned(yf)

    for k, frm in da_keys:
        arrive(k, da_in.at[pl.ds(2 * frm, 2)])

    def cot(i, carry):
        rows = rows_of(i)
        dd = da_in[pl.ds(2 * i, 2)].reshape(256, 128).astype(F32)
        prod = dd * attn[pl.ds(2 * i, 2)].reshape(256, 128).astype(F32)
        for h in (0, 1):
            iv = inv[h, rows]
            mine = first if h == 0 else ~first
            delta = jnp.sum(jnp.where(mine, prod, 0.0), -1, keepdims=True) * iv
            hi = delta.astype(BF16).astype(F32)
            lo = delta - hi
            at = 64 if h == 0 else 0
            e = jnp.where(mine, dd * iv, jnp.where(lane == at, -hi, jnp.where(lane == at + 1, -lo, 0.0)))
            ext[h, rows] = e.astype(BF16)
        return carry

    lax.fori_loop(0, 4, cot, 0)
    dvs = []
    for h in (0, 1):
        e_t = ext[h].T
        dvs.append(dot(e_t[64 * h:64 * h + 64], p_all[h]))
    gp[:, :, 0:128] = jnp.concatenate(dvs, 0).T.astype(BF16).reshape(8, 128, 128)
    v_keys = spread(gp, g_in, 0)
    zc.step(2)

    def weight_grad(lo, to):
        res = dot(n_t[...], gp[:, :, lo:lo + 128].reshape(1024, 128))
        gw_f[:, :, :, to:to + 128] = res.reshape(16, 2, 32, 128)
        gw_b[:, :, :, to:to + 128] = res.astype(BF16).reshape(16, 2, 32, 128)

    def out_grad_send():
        for i in range(4):
            go = dot(g_t[...], a_in[i].reshape(256, 128)).reshape(16, 2, 32, 128)
            go_f[i] = go
            go_b[i] = go.astype(BF16)
        return push(go_b.at[:, :, 1 - core], go_sib, sib)

    def out_far_send(k):
        arrive(k, go_sib)
        for i in range(4):
            go_f[i, :, core] = go_f[i, :, core] + go_sib[i].astype(F32)
        go_send[2] = go_f[2, :, core].astype(BF16)
        return (
            push(go_send.at[2, 0:8], go_half.at[0], up),
            push(go_send.at[2, 8:16], go_half.at[1], down),
        )

    def out_grad_on(keys):
        arrive(keys[0], go_half.at[0])
        arrive(keys[1], go_half.at[1])
        go_send[0, 0:8] = (go_f[1, 0:8, core] + go_half[0].astype(F32)).astype(BF16)
        go_send[0, 8:16] = go_f[1, 8:16, core].astype(BF16)
        go_send[1, 0:8] = go_f[3, 0:8, core].astype(BF16)
        go_send[1, 8:16] = (go_f[3, 8:16, core] + go_half[1].astype(F32)).astype(BF16)
        return push(go_send.at[0], go_in.at[0], up), push(go_send.at[1], go_in.at[1], down)

    def out_grad(keys):
        arrive(keys[0], go_in.at[0])
        arrive(keys[1], go_in.at[1])
        tot = go_f[0, :, core] + go_in[0].astype(F32) + go_in[1].astype(F32)
        gw_f[:, core, :, 256:384] = tot
        gw_sum[:, :, 256:384] = tot.astype(BF16)

    def pair_send(lo, hi):
        return push(gw_b.at[:, 1 - core, :, lo:hi], gw_sib.at[:, :, lo:hi], sib)

    def reduce_send(k, lo, hi, start):
        arrive(k, gw_sib.at[:, :, lo:hi])
        tot = gw_f[:, core, :, lo:hi] + gw_sib[:, :, lo:hi].astype(F32)
        gw_f[:, core, :, lo:hi] = tot
        gw_sum[:, :, lo:hi] = tot.astype(BF16)
        keys = []
        for dz in (4, 3, 5, 2, 6, 1, 7, 0):
            for dx in (1, 0):
                if dx or dz:
                    to = ((xh + dx) % 2) * 8 + (z + dz) % 8
                    frm = ((xh + dx) % 2) * 8 + (z + 8 - dz) % 8
                    dev = {"rows": to * 2 + core, "cols": c}
                    keys.append(
                        (push(gw_sum.at[to, :, start:hi], gw_in.at[m16, :, start:hi], dev), frm)
                    )
        return keys

    def reduce_done(keys, lo, hi):
        tot = gw_f[m16, core, :, lo:hi]
        for k, frm in keys:
            arrive(k, gw_in.at[frm, :, lo:hi])
            tot = tot + gw_in[frm, :, lo:hi].astype(F32)
        return tot

    def turned_rows(into, lo, hi):
        return [
            jnp.concatenate([into[yy, 1 - xl, :, lo:hi], into[yy, xl, :, lo:hi]], 0).T
            for yy in range(4)
        ]

    def terms(turned_in, nb, lo, hi, own, others):
        acc = None
        parts = slice(4 * (nb % 2), 4 * (nb % 2) + 4)
        for yy in range(4):
            rows = (nb // 2, parts)
            if yy:
                w = others[yy - 1, rows[0], rows[1], :, :, lo:hi].reshape(256, hi - lo)
            else:
                p, q = OWN[lo, hi]
                w = own[0, rows[0], rows[1], :, :, p:q].reshape(256, q - p)
            t = dot(w, turned_in[yy])
            acc = t if acc is None else acc + t
        return acc

    gathered(a_keys, a_in, 0)
    k_go = out_grad_send()
    a_turned = turned_rows(a_in, 0, 128)
    for nb in range(4):
        acc = terms(a_turned, nb, 0, 128, wa, wb).T
        part_send[0, nb] = acc[:128].astype(BF16)
        part_own[0, :, 256 * nb:256 * nb + 256] = acc[128:]
    k_out = push(part_send.at[0], part_in.at[0], side)
    go_keys = out_far_send(k_go)
    weight_grad(0, 0)
    zc.step(3)

    def backward_head(h, between=None):
        dk_t[...] = jnp.zeros_like(dk_t)

        def one(i, carry):
            rows = pl.ds(i * 512, 512)
            dpd = dot(ext[h, rows], v_t[h])
            ds = (p_all[h, rows].astype(F32) * dpd).astype(BF16)
            dq_t[:, rows] = dot(ds, kq[h]).T[:64]
            dk_t[...] += dot(kq_t[h, 64:128, rows], ds)
            return carry

        one(0, 0)
        got = between() if between else None
        one(1, 0)

        def maps(i, carry):
            rows = rows_of(i)
            d = jnp.stack([dk_t[:, rows] * (1.0 / LOG2E), dq_t[:, rows]])
            u = u_t[h, :, :, rows]
            d = r_t[h, :, :, rows] * (d - u * jnp.sum(u * d, 1, keepdims=True))
            gp[pl.ds(2 * i, 2), :, 128 + 128 * h:256 + 128 * h] = (
                d.reshape(128, 256).T.astype(BF16).reshape(2, 128, 128)
            )
            return carry

        lax.fori_loop(0, 4, maps, 0)
        return got

    go_keys = backward_head(0, lambda: out_grad_on(go_keys))
    h0_keys = spread(gp, g_in, 128)
    zc.last()
    weight_grad(128, 128)
    k_pair0 = pair_send(0, 256)

    def meanwhile():
        return reduce_send(k_pair0, 0, 256, 0)

    rs0 = backward_head(1, meanwhile)
    h1_keys = spread(gp, g_in, 256)
    weight_grad(256, 384)
    k_pair1 = pair_send(384, 512)
    out_grad(go_keys)

    gathered(v_keys, g_in, 0)
    gathered(h0_keys, g_in, 128)
    zc.finish()
    g_turned = turned_rows(g_in, 0, 256)
    for nb in range(4):
        held[nb] = terms(g_turned, nb, 0, 256, wa, wc)
    rs1 = reduce_send(k_pair1, 384, 512, 256)
    gathered(h1_keys, g_in, 256)
    back = []
    g_turned = turned_rows(g_in, 256, 384)
    for nb in range(4):
        acc = (held[nb] + terms(g_turned, nb, 256, 384, wa, wc)).T
        part_send[1, nb] = acc[:128].astype(BF16)
        part_own[1, :, 256 * nb:256 * nb + 256] = acc[128:]
        back.append(push(part_send.at[1, nb], part_in.at[1, nb], side))

    def whole(which):
        return jnp.concatenate([part_in[which, nb] for nb in range(4)], -1).astype(F32)

    arrive(k_out, part_in.at[0])
    xf = xs[...]
    out_ref[0] = (xf + part_own[0] + whole(0)).reshape(32, 4, 1024).astype(BF16)
    got = reduce_done(rs0, 0, 256)
    gqkv_ref[2] = got[:, 0:128]
    got0 = got[:, 128:256]
    for nb in range(4):
        arrive(back[nb], part_in.at[1, nb])
    dn = (part_own[1] + whole(1)) * gain
    inner = jnp.mean(xf * dn, -1, keepdims=True)
    rs = lax.rsqrt(jnp.mean(xf * xf, -1, keepdims=True) + EPS)
    gt = g_two[xl].astype(F32) + rs * (dn - xf * (rs * rs * inner))
    gtok_ref[0] = gt.reshape(32, 4, 1024).astype(BF16)
    got1 = reduce_done(rs1, 256, 512)
    gout_ref[...] = got1[:, 0:128]
    got1 = got1[:, 128:256]
    gqkv_ref[0] = jnp.concatenate([got0[:, 64:], got1[:, 64:]], -1)
    gqkv_ref[1] = jnp.concatenate([got0[:, :64], got1[:, :64]], -1)
    for d in sends:
        d.wait_send()
    assert count[0] <= NSEM


def hand_on(*refs):
    for src, dst in zip(refs[:4], refs[4:]):
        dst[...] = src[...]


def per_device(image_tokens, cotangent, noise_level, cond_table, head_scale, w_qkv, w_out):
    hbm = pl.BlockSpec(memory_space=pl.ANY)
    vm = pl.BlockSpec(memory_space=pltpu.VMEM)
    sm = pl.BlockSpec(memory_space=pltpu.SMEM)
    V = pltpu.VMEM
    out, gtok, gqkv, gout = pl.pallas_call(
        kernel,
        out_shape=(
            jax.ShapeDtypeStruct((1, 32, 4, 1024), BF16),
            jax.ShapeDtypeStruct((1, 32, 4, 1024), BF16),
            jax.ShapeDtypeStruct((3, 32, 128), F32),
            jax.ShapeDtypeStruct((32, 128), F32),
        ),
        in_specs=[sm, sm, hbm, hbm, hbm, vm, vm],
        out_specs=[vm, vm, vm, vm],
        scratch_shapes=[
            V((128, 1024), F32),
            V((8, 2, 4, 16, 1024), BF16),
            V((2, 128, 1024), BF16),
            V((1024, 1024), BF16),
            V((1, 2, 8, 2, 32, 512), BF16),
            V((3, 2, 8, 2, 32, 128), BF16),
            V((3, 2, 8, 2, 32, 384), BF16),
            V((2, 2, 64, 1024), F32),
            V((2, 2, 1, 1024), F32),
            V((2, 128, 1024), BF16),
            V((2, 128, 1024), BF16),
            V((2, 1024, 128), BF16),
            V((2, 1024, 128), BF16),
            V((2, 128, 1024), BF16),
            V((2, 1024, 1024), BF16),
            V((8, 128, 128), BF16),
            V((2, 1024, 1), F32),
            V((2, 1024, 128), BF16),
            V((4, 2, 128, 128), BF16),
            V((8, 128, 128), BF16),
            V((1024, 256), BF16),
            V((4, 16, 2, 32, 128), F32),
            V((4, 16, 2, 32, 128), BF16),
            V((4, 16, 32, 128), BF16),
            V((3, 16, 32, 128), BF16),
            V((2, 8, 32, 128), BF16),
            V((2, 16, 32, 128), BF16),
            V((64, 1024), F32),
            V((64, 1024), F32),
            V((8, 128, 384), BF16),
            V((4, 2, 128, 128), BF16),
            V((4, 2, 128, 384), BF16),
            V((2, 128, 1024), F32),
            V((2, 4, 128, 256), BF16),
            V((2, 4, 128, 256), BF16),
            V((16, 2, 32, 512), F32),
            V((16, 2, 32, 512), BF16),
            V((16, 32, 512), BF16),
            V((16, 32, 512), BF16),
            V((16, 32, 512), BF16),
            V((4, 256, 256), F32),
            V((32, 4, 1024), BF16),
            V((32, 4, 1024), BF16),
            V((256, 1024), F32),
            pltpu.SemaphoreType.DMA((NSEM,)),
            pltpu.SemaphoreType.DMA((NSEM,)),
            pltpu.SemaphoreType.DMA((3,)),
        ],
        compiler_params=pltpu.CompilerParams(
            collective_id=0, has_side_effects=True, vmem_limit_bytes=56 * 1024 * 1024
        ),
        cost_estimate=pl.CostEstimate(
            flops=4_800_000_000, bytes_accessed=4_000_000, transcendentals=2_200_000
        ),
    )(noise_level, head_scale, image_tokens, cotangent, cond_table, w_qkv, w_out.T)
    got = (out, gtok, gqkv, gout)
    out, gtok, gqkv, gout = pl.pallas_call(
        hand_on,
        out_shape=tuple(jax.ShapeDtypeStruct(a.shape, a.dtype) for a in got),
        in_specs=[vm] * 4,
        out_specs=[vm] * 4,
    )(*got)
    return out, gtok, gqkv, gout.T


def solution(mesh):
    return jax.shard_map(
        per_device,
        mesh=mesh,
        in_specs=(
            P("rows", None, "cols", None),
            P("rows", None, "cols", None),
            P("rows"),
            P(),
            P(),
            P(None, "rows", "cols"),
            P("cols", "rows"),
        ),
        out_specs=(
            P("rows", None, "cols", None),
            P("rows", None, "cols", None),
            P(None, "rows", "cols"),
            P("cols", "rows"),
        ),
        check_vma=False,
    )
```
